32 devices in a mesh: seq: 8 (over z, x), doc: 4 (over y, core).
Axes of the slice: x: 2, y: 2, z: 4, core: 2. Of those that a mesh axis runs over, the one named last changes fastest.
Arguments:
- inputs: bfloat16 [4096, 1024], P('seq', 'doc'), may hold values from -4 to 4
- queries: bfloat16 [4096, 1024], P('seq', 'doc'), may hold values from -128 to 128
- keys_values: bfloat16 [2, 4096, 1024], P(None, 'seq', 'doc'), may hold values from -10 to 10
- slot_weight: bfloat16 [1024, 4096], P(None, 'doc'), may hold values from -3 to 3
- slot_gain: float32 [2, 1024], P(None, 'doc'), may hold values from 0.1 to 1.9
- slot_bias: float32 [2, 1024], P(None, 'doc'), may hold values from -3 to 3
- bounds: int32 [2, 4096], P(None, 'seq'), may hold values from 0 to 4096, as said below
Outputs:
- attended: bfloat16 [4096, 1024], P('seq', 'doc')
The draws below stay inside these ranges and needn't reach their ends.
Inputs may be any that keep to these rules, and one draw needn't show every extreme that they name: The sequence holds exactly 2 documents in order, the first starting at 0 and each of 1024 tokens or more: bounds[0, i] <= i < bounds[1, i], and every token of a document has the same pair.
All inputs are finite; a program needn't handle non-finite values.
Results may differ from the reference program's by a relative error of at most 0.0045.
Values may be sent and summed in bfloat16 or wider, within the bound.
A program may use at most 64 MiB of HBM per device.

```python
import math
import jax
import jax.numpy as jnp
from jax import lax

H = 16
DH = 64
R = 256
W = 128
DOCS = 2
D = 1024
TOKENS = 4096


def draw_inputs(key, part):
    drawn = jax.random.truncated_normal(jax.random.fold_in(key, 21), -4.0, 4.0, (TOKENS, D))
    return drawn.astype(jnp.bfloat16)


def draw_slot_weight(key, part):
    drawn = 0.0625 * jax.random.truncated_normal(jax.random.fold_in(key, 22), -4.0, 4.0, (D, H * R))
    return drawn.astype(jnp.bfloat16)


def draw_keys_values(key, part):
    drawn = jax.random.truncated_normal(jax.random.fold_in(key, 23), -4.0, 4.0, (2, TOKENS, D))
    return drawn.astype(jnp.bfloat16)


def draw_queries(key, part):
    drawn = 1.2 * jax.random.truncated_normal(jax.random.fold_in(key, 24), -4.0, 4.0, (TOKENS, D))
    return drawn.astype(jnp.bfloat16)


def draw_bounds(key, part):
    places = jnp.arange(TOKENS, dtype=jnp.int32)
    split_at = jax.random.randint(jax.random.fold_in(key, 31), (), TOKENS // 4, TOKENS - TOKENS // 4 + 1)
    later = places >= split_at
    starts = jnp.where(later, split_at, 0)
    doc_end = jnp.where(later, TOKENS, split_at)
    return jnp.stack([starts, doc_end]).astype(jnp.int32)


def steps_of(stream_key, dims, cuts, low, top_value):
    def one(position, shards_of):
        steps = jax.random.uniform(jax.random.fold_in(jax.random.fold_in(stream_key, 6), position), (shards_of,), jnp.float32, low / len(cuts), top_value / len(cuts))
        return jnp.repeat(jnp.exp(steps), dims[position] // shards_of).reshape((-1,) + (1,) * (len(dims) - position - 1))

    level = one(*cuts[0])
    for cut in cuts[1:]:
        level = level * one(*cut)
    return level


def normal_values(key, shape, width, bound, shards=(), held_as=jnp.bfloat16):
    values = width * jax.random.normal(key, shape, jnp.float32)
    if shards:
        values = values * steps_of(key, shape, shards, -0.22, 0.18)
    return jnp.clip(values, -bound, bound).astype(held_as)


def setup_inputs(seed: int = 0) -> dict:
    key_of = jax.random.split(jax.random.key(seed), 8)
    inputs = draw_inputs(jax.random.fold_in(key_of[7], 71), 0)
    queries = draw_queries(jax.random.fold_in(key_of[7], 71), 0)
    keys_values = draw_keys_values(jax.random.fold_in(key_of[7], 71), 0)
    slot_weight = draw_slot_weight(jax.random.fold_in(key_of[7], 71), 0)
    slot_gain = jnp.clip(1.0 + 0.18 * jax.random.normal(key_of[4], (2, D), jnp.float32), 0.1, 1.9)
    slot_bias = normal_values(key_of[5], (2, D), 0.5, 3.0, ((1, 4),), jnp.float32)
    bounds = draw_bounds(jax.random.fold_in(key_of[7], 71), 0)
    return dict(inputs=inputs, queries=queries, keys_values=keys_values, slot_weight=slot_weight, slot_gain=slot_gain, slot_bias=slot_bias, bounds=bounds)


epsilon = 1e-05

def normalize(numerator, gain, bias):
    mean_val = lax.optimization_barrier(jnp.mean(numerator, axis=-1, keepdims=True))
    centred = numerator - mean_val
    variance = lax.optimization_barrier(jnp.mean(centred * centred, axis=-1, keepdims=True))
    return centred * lax.rsqrt(variance + epsilon) * gain + bias

def attend(query_block, window, lower, upper, first_pos, slot_keys, slot_values):
    q_len = query_block.shape[0]
    k_len = window.shape[1]
    second = (lower > 0)[None, :, None]
    near_scores = jnp.einsum('qhe,khe->hqk', query_block, window[0]) * 0.125
    far_all = jnp.einsum('qhe,ghre->ghqr', query_block, slot_keys) * 0.125
    far_scores = jnp.where(second, far_all[1], far_all[0])
    query_pos = first_pos + jnp.arange(q_len, dtype=jnp.int32)
    key_pos = first_pos - W + jnp.arange(k_len, dtype=jnp.int32)
    offset = key_pos[None, :] - query_pos[:, None]
    allowed = (jnp.abs(offset) <= W) & (key_pos[None, :] >= lower[:, None]) & (key_pos[None, :] < upper[:, None])
    near_scores = jnp.where(allowed[None], near_scores, -jnp.inf)
    row_top = jnp.maximum(lax.optimization_barrier(jnp.max(near_scores, axis=-1)), lax.optimization_barrier(jnp.max(far_scores, axis=-1)))
    near_weight = jnp.exp(near_scores - row_top[..., None])
    far_weight = jnp.exp(far_scores - row_top[..., None])
    row_total = lax.optimization_barrier(jnp.sum(near_weight, axis=-1)) + lax.optimization_barrier(jnp.sum(far_weight, axis=-1))
    near_b = lax.optimization_barrier(near_weight.astype(jnp.bfloat16)).astype(jnp.float32)
    far_b = lax.optimization_barrier(far_weight.astype(jnp.bfloat16)).astype(jnp.float32)
    zero_val = jnp.zeros((), jnp.float32)
    result = jnp.einsum('hqk,khe->qhe', near_b, window[1])
    result = result + jnp.einsum('hqr,hre->qhe', jnp.where(second, zero_val, far_b), slot_values[0])
    result = result + jnp.einsum('hqr,hre->qhe', jnp.where(second, far_b, zero_val), slot_values[1])
    result = result / jnp.transpose(row_total)[:, :, None]
    return result.reshape(q_len, H * DH).astype(jnp.bfloat16)

def reference(inputs, queries, keys_values, slot_weight, slot_gain, slot_bias, bounds):
    blk_len = math.gcd(TOKENS, 4096)
    blk_count = TOKENS // blk_len
    blocks = jnp.arange(blk_count, dtype=jnp.int32)
    doc_ids = (bounds[0] > 0).astype(jnp.int32)

    def block_logits(block_at):
        feature_rows = lax.dynamic_slice_in_dim(inputs, block_at * blk_len, blk_len, 0)
        return jnp.dot(feature_rows, slot_weight, preferred_element_type=jnp.float32)

    def block_docs(block_at):
        return lax.dynamic_slice_in_dim(doc_ids, block_at * blk_len, blk_len, 0)

    def top_step(running, block_at):
        logits = block_logits(block_at)
        owner = block_docs(block_at)
        first = lax.optimization_barrier(jnp.max(jnp.where((owner == 0)[:, None], logits, -jnp.inf), axis=0))
        other = lax.optimization_barrier(jnp.max(jnp.where((owner == 1)[:, None], logits, -jnp.inf), axis=0))
        return (jnp.maximum(running, jnp.stack([first, other])), None)
    slot_top, _ = lax.scan(top_step, jnp.full((DOCS, H * R), -jnp.inf, jnp.float32), blocks)

    def sum_step(running, block_at):
        owner = block_docs(block_at)
        top_rows = jnp.where((owner == 1)[:, None], slot_top[1][None, :], slot_top[0][None, :])
        proj = lax.optimization_barrier(jnp.exp(block_logits(block_at) - top_rows).astype(jnp.bfloat16))
        proj = proj.astype(jnp.float32).reshape(blk_len, H, R)
        picks = jnp.stack([owner == 0, owner == 1]).astype(jnp.float32)
        kv_pair = lax.dynamic_slice_in_dim(keys_values, block_at * blk_len, blk_len, 1).astype(jnp.float32)
        kv_pair = kv_pair.reshape(2, blk_len, H, DH)
        return (running + jnp.einsum('gt,thr,stha->ghrsa', picks, proj, kv_pair), None)
    numerator, _ = lax.scan(sum_step, jnp.zeros((DOCS, H, R, 2, DH), jnp.float32), blocks)
    gain = jnp.transpose(slot_gain.reshape(2, H, DH), (1, 0, 2))[None, :, None]
    bias = jnp.transpose(slot_bias.reshape(2, H, DH), (1, 0, 2))[None, :, None]
    slot_table = normalize(numerator, gain, bias).astype(jnp.bfloat16).astype(jnp.float32)
    slot_keys = slot_table[:, :, :, 0]
    slot_values = slot_table[:, :, :, 1]
    q_len = math.gcd(TOKENS, 512)
    padded = jnp.pad(keys_values, ((0, 0), (W, W), (0, 0)))

    def one_block(block_at):
        start_at = block_at * q_len
        query_block = lax.dynamic_slice_in_dim(queries, start_at, q_len, 0).astype(jnp.float32).reshape(q_len, H, DH)
        window = lax.dynamic_slice_in_dim(padded, start_at, q_len + 2 * W, 1).astype(jnp.float32)
        window = window.reshape(2, q_len + 2 * W, H, DH)
        lower = lax.dynamic_slice_in_dim(bounds[0], start_at, q_len, 0)
        upper = lax.dynamic_slice_in_dim(bounds[1], start_at, q_len, 0)
        return attend(query_block, window, lower, upper, start_at, slot_keys, slot_values)
    outputs = lax.map(one_block, jnp.arange(TOKENS // q_len, dtype=jnp.int32))
    return outputs.reshape(TOKENS, H * DH)
```

```python
import functools

import jax
import jax.numpy as jnp
from jax import lax
from jax.experimental import pallas as pl
from jax.experimental.pallas import tpu as pltpu
from jax.sharding import PartitionSpec as P

DH = 64
R = 256
W = 128
DOCS = 2
CHUNKS = 2
EPSILON = 1e-05
LOW = -1e30
MESH = pl.DeviceIdType.MESH
F32 = jnp.float32
BF16 = jnp.bfloat16

NT = (((1,), (1,)), ((), ()))


def kernel(
    n, nd,
    x_ref, q_ref, kv_ref, w_ref, gain_ref, bias_ref, bounds_ref,
    out_ref,
    xg, wv, qv, kvx, kvm, acc, part, tops, rbuf, rtop, tab,
    gcol, bcol, nbias, nacc, nmax, nsum,
    loc_sem, far_send, far_recv, pair_send, pair_recv, fwd_send, fwd_recv,
    halo_send, halo_recv, part_send, part_recv, top_send, top_recv,
    tab_send, tab_recv,
):
    T, F = x_ref.shape
    heads = q_ref.shape[1] // DH
    blocks = DOCS * heads
    stride = n // blocks
    me = lax.axis_index("seq")
    c = lax.axis_index("doc")
    pc = c + 1 - 2 * lax.rem(c, 2)
    rows = T // CHUNKS

    barrier = pltpu.get_barrier_semaphore()

    def greet(d, carry):
        pl.semaphore_signal(
            barrier, inc=1, device_id={"seq": lax.rem(me + d, n), "doc": c}, device_id_type=MESH
        )
        return carry

    lax.fori_loop(1, n, greet, 0)
    for d in range(1, nd):
        pl.semaphore_signal(
            barrier, inc=1, device_id={"seq": me, "doc": lax.rem(c + d, nd)}, device_id_type=MESH
        )

    cp_x = pltpu.make_async_copy(x_ref, xg.at[c], loc_sem.at[0])
    cp_w = pltpu.make_async_copy(w_ref, wv, loc_sem.at[1])
    cp_q = pltpu.make_async_copy(q_ref, qv, loc_sem.at[2])
    cp_kv = pltpu.make_async_copy(kv_ref, kvx.at[:, pl.ds(W, T), :], loc_sem.at[3])
    for cp in (cp_x, cp_w, cp_kv, cp_q):
        cp.start()

    pl.semaphore_wait(barrier, n - 1 + nd - 1)

    def remote(src, dst, send, recv, seq, doc):
        return pltpu.make_async_remote_copy(
            src_ref=src, dst_ref=dst, send_sem=send, recv_sem=recv,
            device_id={"seq": seq, "doc": doc}, device_id_type=MESH,
        )

    far = []
    for k in range(1, nd // 2):
        for j in range(CHUNKS):
            part_rows = pl.ds(j * rows, rows)
            cp = remote(
                x_ref.at[part_rows], xg.at[c, part_rows],
                far_send.at[k, j], far_recv.at[k, j], me, lax.rem(c + 2 * k, nd),
            )
            cp.start()
            far.append((k, j, cp))
    cp_pair = remote(x_ref, xg.at[c], pair_send, pair_recv, me, pc)
    cp_pair.start()

    up = remote(
        kv_ref.at[:, pl.ds(T - W, W), :], kvx.at[:, pl.ds(0, W), :],
        halo_send.at[0], halo_recv.at[0], lax.rem(me + 1, n), c,
    )
    down = remote(
        kv_ref.at[:, pl.ds(0, W), :], kvx.at[:, pl.ds(T + W, W), :],
        halo_send.at[1], halo_recv.at[1], lax.rem(me + n - 1, n), c,
    )

    @pl.when(me < n - 1)
    def _():
        up.start()

    @pl.when(me > 0)
    def _():
        down.start()

    @pl.when(me == 0)
    def _():
        kvx[:, 0:W, :] = jnp.zeros((2, W, F), BF16)

    @pl.when(me == n - 1)
    def _():
        kvx[:, T + W : T + 2 * W, :] = jnp.zeros((2, W, F), BF16)

    lower = bounds_ref[0, 0]
    split = jnp.where(lower > 0, lower, bounds_ref[1, 0])
    root = me * T
    row_pos = root + lax.broadcasted_iota(jnp.int32, (T, 1), 0)
    second = row_pos >= split

    def w_rows(i):
        return wv[pl.ds(pl.multiple_of(i * F, F), F), :]

    cp_x.wait()
    cp_w.wait()
    acc[...] = jnp.dot(xg[c], w_rows(c), preferred_element_type=F32)
    cp_pair.wait_recv()
    acc[...] += jnp.dot(xg[pc], w_rows(pc), preferred_element_type=F32)

    cp_kv.wait()
    lane_pos = root + lax.broadcasted_iota(jnp.int32, (1, T), 1)
    lane_second = lane_pos >= split
    for s in range(2):
        turned = jnp.transpose(kvx[s, W : W + T, :].astype(F32))
        first_doc = jnp.where(lane_second, 0.0, turned).astype(BF16)
        other_doc = jnp.where(lane_second, turned, 0.0).astype(BF16)
        for h in range(heads):
            kvm[h, 0, s] = first_doc[h * DH : (h + 1) * DH]
            kvm[h, 1, s] = other_doc[h * DH : (h + 1) * DH]

    fwd = []
    for k, j, cp in far:
        cp.wait_recv()
        src = lax.rem(c - 2 * k + nd, nd)
        part_rows = pl.ds(j * rows, rows)
        cp2 = remote(
            xg.at[src, part_rows], xg.at[src, part_rows],
            fwd_send.at[k, j], fwd_recv.at[k, j], me, pc,
        )
        cp2.start()
        fwd.append(cp2)
    for k in range(1, nd // 2):
        src = lax.rem(c - 2 * k + nd, nd)
        acc[...] += jnp.dot(xg[src], w_rows(src), preferred_element_type=F32)
    for cp2 in fwd:
        cp2.wait_recv()
    for k in range(1, nd // 2):
        src = lax.rem(pc - 2 * k + nd, nd)
        acc[...] += jnp.dot(xg[src], w_rows(src), preferred_element_type=F32)

    sends = []
    for h in range(heads):
        logits = acc[:, h * R : (h + 1) * R]
        top0 = jnp.max(jnp.where(second, LOW, logits), axis=0, keepdims=True)
        top1 = jnp.max(jnp.where(second, logits, LOW), axis=0, keepdims=True)
        proj = jnp.exp(logits - jnp.where(second, top1, top0)).astype(BF16)
        sums = jnp.dot(
            kvm[h].reshape(DOCS * 2 * DH, T), proj, preferred_element_type=F32
        ).reshape(DOCS, 2, DH, R)
        sums = sums - jnp.mean(sums, axis=2, keepdims=True)
        for g, top in ((0, top0), (1, top1)):
            b = g * heads + h
            owner = b * stride
            slot = lax.rem(me - owner + n, n)
            tops[b] = jnp.broadcast_to(top, (8, R))
            part[b] = sums[g].astype(BF16)
            send_top = remote(
                tops.at[b], rtop.at[slot], top_send.at[b], top_recv.at[slot], owner, c
            )
            send_part = remote(
                part.at[b], rbuf.at[slot], part_send.at[b], part_recv.at[slot], owner, c
            )
            sends.append((owner, send_top, send_part))

            @pl.when(me != owner)
            def _():
                send_top.start()
                send_part.start()

    diagonal = lax.broadcasted_iota(jnp.int32, (F, F), 0) == lax.broadcasted_iota(
        jnp.int32, (F, F), 1
    )
    for s in range(2):
        for ref, col in ((gain_ref, gcol), (bias_ref, bcol)):
            value = jnp.sum(jnp.where(diagonal, ref[s : s + 1, :], 0.0), axis=1, keepdims=True)
            col[s] = jnp.broadcast_to(value, (F, 128))

    total = n * T
    for b in range(T // W):
        q_pos = root + b * W + lax.broadcasted_iota(jnp.int32, (W, 3 * W), 0)
        k_pos = root + (b - 1) * W + lax.broadcasted_iota(jnp.int32, (W, 3 * W), 1)
        low = jnp.maximum(q_pos - W, jnp.where(q_pos >= split, split, 0))
        high = jnp.minimum(q_pos + W + 1, jnp.where(q_pos >= split, total, split))
        nbias[b] = jnp.where((k_pos >= low) & (k_pos < high), 0.0, LOW)

    cp_q.wait()

    @pl.when(me > 0)
    def _():
        up.wait_recv()

    @pl.when(me < n - 1)
    def _():
        down.wait_recv()

    half = lax.broadcasted_iota(jnp.int32, (1, 2 * DH), 1) // DH

    def query(h, start, size):
        p = h // 2
        q = qv[start : start + size, p * 2 * DH : (p + 1) * 2 * DH] * jnp.asarray(0.125, BF16)
        return jnp.where(half == h % 2, q, jnp.zeros((), BF16))

    def near(h):
        p = h // 2
        lanes = slice(p * 2 * DH, (p + 1) * 2 * DH)
        for b in range(T // W):
            keys = kvx[0, b * W : (b + 3) * W, lanes]
            values = kvx[1, b * W : (b + 3) * W, lanes]
            scores = lax.dot_general(query(h, b * W, W), keys, NT, preferred_element_type=F32)
            scores = scores + nbias[b]
            top = jnp.max(scores, axis=1, keepdims=True)
            weight = jnp.exp(scores - top)
            at = slice(b * W, (b + 1) * W)
            nmax[h, at] = top
            nsum[h, at] = jnp.sum(weight, axis=1, keepdims=True)
            nacc[h, at] = jnp.dot(weight.astype(BF16), values, preferred_element_type=F32)

    for h in range(heads // 2):
        near(h)

    mine = me // stride

    def reduce_block():
        rbuf[0] = part[mine]
        rtop[0] = tops[mine]

        def wait_in(d, top):
            remote(
                tops.at[0], rtop.at[d], top_send.at[0], top_recv.at[d], me, pc
            ).wait_recv()
            remote(
                part.at[0], rbuf.at[d], part_send.at[0], part_recv.at[d], me, pc
            ).wait_recv()
            return jnp.maximum(top, rtop[d])

        top = lax.fori_loop(1, n, wait_in, rtop[0], unroll=n <= 8)[0:1]

        def add(d, running):
            scale = jnp.exp(rtop[d][0:1] - top)
            return running + rbuf[d].astype(F32) * scale[None]

        summed = lax.fori_loop(0, n, add, jnp.zeros((2, DH, R), F32), unroll=n <= 8)
        centred = summed - jnp.mean(summed, axis=1, keepdims=True)
        variance = jnp.mean(centred * centred, axis=1, keepdims=True)
        scaled = centred * lax.rsqrt(variance + EPSILON)
        at = pl.ds(pl.multiple_of(lax.rem(mine, heads) * DH, DH), DH)
        for s in range(2):
            gain = gcol[s, at, :][:, 0:1]
            bias = bcol[s, at, :][:, 0:1]
            tab[mine, s] = (scaled[s] * gain + bias).astype(BF16)

        def spread(d, carry):
            remote(
                tab.at[mine], tab.at[mine], tab_send.at[d], tab_recv.at[mine],
                lax.rem(me + d, n), c,
            ).start()
            return carry

        lax.fori_loop(1, n, spread, 0)

    def finish_spread():
        def done(d, carry):
            remote(
                tab.at[mine], tab.at[mine], tab_send.at[d], tab_recv.at[mine],
                lax.rem(me + d, n), c,
            ).wait_send()
            return carry

        lax.fori_loop(1, n, done, 0)

    if stride == 1 and n == blocks:
        reduce_block()
    else:
        pl.when((lax.rem(me, stride) == 0) & (mine < blocks))(reduce_block)

    for h in range(heads // 2, heads):
        near(h)

    for b in range(blocks):
        @pl.when(me != b * stride)
        def _():
            remote(
                tab.at[b], tab.at[b], tab_send.at[0], tab_recv.at[b], me, pc
            ).wait_recv()

    for p in range(heads // 2):
        keys = [
            tab[g * heads + 2 * p : g * heads + 2 * p + 2, 0].reshape(2 * DH, R)
            for g in range(DOCS)
        ]
        values = [
            tab[g * heads + 2 * p : g * heads + 2 * p + 2, 1].reshape(2 * DH, R)
            for g in range(DOCS)
        ]
        halves = []
        for h in (2 * p, 2 * p + 1):
            q = query(h, 0, T)
            scores = jnp.where(
                second,
                jnp.dot(q, keys[1], preferred_element_type=F32),
                jnp.dot(q, keys[0], preferred_element_type=F32),
            )
            near_top = nmax[h]
            top = jnp.maximum(near_top, jnp.max(scores, axis=1, keepdims=True))
            weight = jnp.exp(scores - top)
            shrink = jnp.exp(near_top - top)
            denominator = nsum[h] * shrink + jnp.sum(weight, axis=1, keepdims=True)
            weight = weight.astype(BF16)
            zero = jnp.zeros((), BF16)
            result = nacc[h] * shrink
            result += lax.dot_general(
                jnp.where(second, zero, weight), values[0], NT, preferred_element_type=F32
            )
            result += lax.dot_general(
                jnp.where(second, weight, zero), values[1], NT, preferred_element_type=F32
            )
            halves.append(result / denominator)
        out_ref[:, p * 2 * DH : (p + 1) * 2 * DH] = jnp.where(
            half == 0, halves[0], halves[1]
        ).astype(out_ref.dtype)

    for _, _, cp in far:
        cp.wait_send()
    cp_pair.wait_send()
    for cp2 in fwd:
        cp2.wait_send()

    @pl.when(me < n - 1)
    def _():
        up.wait_send()

    @pl.when(me > 0)
    def _():
        down.wait_send()

    for owner, send_top, send_part in sends:
        @pl.when(me != owner)
        def _():
            send_top.wait_send()
            send_part.wait_send()

    if stride == 1 and n == blocks:
        finish_spread()
    else:
        pl.when((lax.rem(me, stride) == 0) & (mine < blocks))(finish_spread)


def on_device(n, nd, inputs, queries, keys_values, slot_weight, slot_gain, slot_bias, bounds):
    T, F = inputs.shape
    heads = queries.shape[1] // DH
    blocks = DOCS * heads
    DMA = pltpu.SemaphoreType.DMA
    anywhere = pl.BlockSpec(memory_space=pl.ANY)
    vmem = pl.BlockSpec(memory_space=pltpu.VMEM)
    return pl.pallas_call(
        functools.partial(kernel, n, nd),
        out_shape=jax.ShapeDtypeStruct(queries.shape, BF16),
        in_specs=[anywhere] * 4 + [vmem] * 2 + [pl.BlockSpec(memory_space=pltpu.SMEM)],
        out_specs=vmem,
        scratch_shapes=[
            pltpu.VMEM((nd, T, F), BF16),
            pltpu.VMEM(slot_weight.shape, BF16),
            pltpu.VMEM(queries.shape, BF16),
            pltpu.VMEM((2, T + 2 * W, F), BF16),
            pltpu.VMEM((heads, DOCS, 2, DH, T), BF16),
            pltpu.VMEM((T, heads * R), F32),
            pltpu.VMEM((blocks, 2, DH, R), BF16),
            pltpu.VMEM((blocks, 8, R), F32),
            pltpu.VMEM((n, 2, DH, R), BF16),
            pltpu.VMEM((n, 8, R), F32),
            pltpu.VMEM((blocks, 2, DH, R), BF16),
            pltpu.VMEM((2, F, 128), F32),
            pltpu.VMEM((2, F, 128), F32),
            pltpu.VMEM((T // W, W, 3 * W), F32),
            pltpu.VMEM((heads, T, 2 * DH), F32),
            pltpu.VMEM((heads, T, 1), F32),
            pltpu.VMEM((heads, T, 1), F32),
            DMA((4,)),
            DMA((nd, CHUNKS)), DMA((nd, CHUNKS)),
            DMA, DMA,
            DMA((nd, CHUNKS)), DMA((nd, CHUNKS)),
            DMA((2,)), DMA((2,)),
            DMA((blocks,)), DMA((n,)),
            DMA((blocks,)), DMA((n,)),
            DMA((n,)), DMA((blocks,)),
        ],
        compiler_params=pltpu.CompilerParams(
            collective_id=0, has_side_effects=True, vmem_limit_bytes=48 * 1024 * 1024
        ),
        cost_estimate=pl.CostEstimate(
            flops=4 * 10**9, bytes_accessed=4 * 10**6, transcendentals=2 * 10**6
        ),
    )(inputs, queries, keys_values, slot_weight, slot_gain, slot_bias, bounds)


def solution(mesh):
    return jax.shard_map(
        functools.partial(on_device, mesh.shape["seq"], mesh.shape["doc"]),
        mesh=mesh,
        in_specs=(
            P("seq", "doc"),
            P("seq", "doc"),
            P(None, "seq", "doc"),
            P(None, "doc"),
            P(None, "doc"),
            P(None, "doc"),
            P(None, "seq"),
        ),
        out_specs=P("seq", "doc"),
        check_vma=False,
    )
```

```python
import functools

import jax
import jax.numpy as jnp
from jax import lax
from jax.experimental import pallas as pl
from jax.experimental.pallas import tpu as pltpu
from jax.sharding import PartitionSpec as P

DH = 64
R = 256
W = 128
DOCS = 2
CHUNKS = 2
EPSILON = 1e-05
LOW = -1e30
MESH = pl.DeviceIdType.MESH
F32 = jnp.float32
BF16 = jnp.bfloat16

NT = (((1,), (1,)), ((), ()))


def kernel(
    n, nd,
    x_ref, q_ref, kv_ref, w_ref, gain_hbm, bias_hbm, bounds_hbm,
    out_ref,
    gain_ref, bias_ref, bounds_ref,
    xg, wv, qv, kvx, kvm, acc, part, tops, rbuf, rtop, tab,
    gcol, bcol, nbias, nacc, nmax, nsum,
    loc_sem, far_send, far_recv, pair_send, pair_recv, fwd_send, fwd_recv,
    halo_send, halo_recv, part_send, part_recv, top_send, top_recv,
    tab_send, tab_recv, hand_send, qdoc,
):
    T, F = x_ref.shape
    heads = q_ref.shape[1] // DH
    blocks = DOCS * heads
    stride = n // blocks
    me = lax.axis_index("seq")
    c = lax.axis_index("doc")
    pc = c + 1 - 2 * lax.rem(c, 2)
    rows = T // CHUNKS

    barrier = pltpu.get_barrier_semaphore()

    def greet(d, carry):
        pl.semaphore_signal(
            barrier, inc=1, device_id={"seq": lax.rem(me + d, n), "doc": c}, device_id_type=MESH
        )
        return carry

    lax.fori_loop(1, n, greet, 0)
    for d in range(1, nd):
        pl.semaphore_signal(
            barrier, inc=1, device_id={"seq": me, "doc": lax.rem(c + d, nd)}, device_id_type=MESH
        )

    cp_x = pltpu.make_async_copy(x_ref, xg.at[c], loc_sem.at[0])
    cp_w = pltpu.make_async_copy(w_ref, wv, loc_sem.at[1])
    cp_q = pltpu.make_async_copy(q_ref, qv, loc_sem.at[2])
    cp_kv = pltpu.make_async_copy(kv_ref, kvx.at[:, pl.ds(W, T), :], loc_sem.at[3])
    cp_bounds = pltpu.make_async_copy(bounds_hbm, bounds_ref, loc_sem.at[4])
    cp_gain = pltpu.make_async_copy(gain_hbm, gain_ref, loc_sem.at[5])
    cp_bias = pltpu.make_async_copy(bias_hbm, bias_ref, loc_sem.at[6])
    for cp in (cp_x, cp_w, cp_bounds, cp_kv, cp_q, cp_gain, cp_bias):
        cp.start()

    pl.semaphore_wait(barrier, n - 1 + nd - 1)

    def remote(src, dst, send, recv, seq, doc):
        return pltpu.make_async_remote_copy(
            src_ref=src, dst_ref=dst, send_sem=send, recv_sem=recv,
            device_id={"seq": seq, "doc": doc}, device_id_type=MESH,
        )

    far = []
    for k in range(1, nd // 2):
        for j in range(CHUNKS):
            part_rows = pl.ds(j * rows, rows)
            cp = remote(
                x_ref.at[part_rows], xg.at[c, part_rows],
                far_send.at[k, j], far_recv.at[k, j], me, lax.rem(c + 2 * k, nd),
            )
            cp.start()
            far.append((k, j, cp))
    cp_pair = remote(x_ref, xg.at[c], pair_send, pair_recv, me, pc)
    cp_pair.start()

    up = remote(
        kv_ref.at[:, pl.ds(T - W, W), :], kvx.at[:, pl.ds(0, W), :],
        halo_send.at[0], halo_recv.at[0], lax.rem(me + 1, n), c,
    )
    down = remote(
        kv_ref.at[:, pl.ds(0, W), :], kvx.at[:, pl.ds(T + W, W), :],
        halo_send.at[1], halo_recv.at[1], lax.rem(me + n - 1, n), c,
    )

    @pl.when(me < n - 1)
    def _():
        up.start()

    @pl.when(me > 0)
    def _():
        down.start()

    @pl.when(me == 0)
    def _():
        kvx[:, 0:W, :] = jnp.zeros((2, W, F), BF16)

    @pl.when(me == n - 1)
    def _():
        kvx[:, T + W : T + 2 * W, :] = jnp.zeros((2, W, F), BF16)

    cp_bounds.wait()
    lower = bounds_ref[0:1, 0:1]
    split = jnp.where(lower > 0, lower, bounds_ref[1:2, 0:1])
    root = me * T
    row_pos = root + lax.broadcasted_iota(jnp.int32, (T, 1), 0)
    second = row_pos >= split

    def w_rows(i):
        return wv[pl.ds(pl.multiple_of(i * F, F), F), :]

    cp_x.wait()
    cp_w.wait()
    acc[...] = jnp.dot(xg[c], w_rows(c), preferred_element_type=F32)
    cp_pair.wait_recv()
    acc[...] += jnp.dot(xg[pc], w_rows(pc), preferred_element_type=F32)

    cp_kv.wait()
    lane_pos = root + lax.broadcasted_iota(jnp.int32, (1, T), 1)
    lane_second = lane_pos >= split
    for s in range(2):
        turned = jnp.transpose(kvx[s, W : W + T, :].astype(F32))
        first_doc = jnp.where(lane_second, 0.0, turned).astype(BF16)
        other_doc = jnp.where(lane_second, turned, 0.0).astype(BF16)
        for h in range(heads):
            kvm[h, 0, s] = first_doc[h * DH : (h + 1) * DH]
            kvm[h, 1, s] = other_doc[h * DH : (h + 1) * DH]

    fwd = []
    for k, j, cp in far:
        cp.wait_recv()
        src = lax.rem(c - 2 * k + nd, nd)
        part_rows = pl.ds(j * rows, rows)
        cp2 = remote(
            xg.at[src, part_rows], xg.at[src, part_rows],
            fwd_send.at[k, j], fwd_recv.at[k, j], me, pc,
        )
        cp2.start()
        fwd.append(cp2)
    for k in range(1, nd // 2):
        src = lax.rem(c - 2 * k + nd, nd)
        acc[...] += jnp.dot(xg[src], w_rows(src), preferred_element_type=F32)
    for cp2 in fwd:
        cp2.wait_recv()
    for k in range(1, nd // 2):
        src = lax.rem(pc - 2 * k + nd, nd)
        acc[...] += jnp.dot(xg[src], w_rows(src), preferred_element_type=F32)

    sends = []
    for h in range(heads):
        logits = acc[:, h * R : (h + 1) * R]
        top0 = jnp.max(jnp.where(second, LOW, logits), axis=0, keepdims=True)
        top1 = jnp.max(jnp.where(second, logits, LOW), axis=0, keepdims=True)
        proj = jnp.exp(logits - jnp.where(second, top1, top0)).astype(BF16)
        sums = jnp.dot(
            kvm[h].reshape(DOCS * 2 * DH, T), proj, preferred_element_type=F32
        ).reshape(DOCS, 2, DH, R)
        sums = sums - jnp.mean(sums, axis=2, keepdims=True)
        for g, top in ((0, top0), (1, top1)):
            b = g * heads + h
            owner = b * stride
            slot = lax.rem(me - owner + n, n)
            tops[b] = jnp.broadcast_to(top, (8, R))
            part[b] = sums[g].astype(BF16)
            send_top = remote(
                tops.at[b], rtop.at[slot], top_send.at[b], top_recv.at[slot], owner, c
            )
            send_part = remote(
                part.at[b], rbuf.at[slot], part_send.at[b], part_recv.at[slot], owner, c
            )
            sends.append((owner, send_top, send_part))

            @pl.when(me != owner)
            def _():
                send_top.start()
                send_part.start()

    cp_gain.wait()
    cp_bias.wait()
    diagonal = lax.broadcasted_iota(jnp.int32, (F, F), 0) == lax.broadcasted_iota(
        jnp.int32, (F, F), 1
    )
    for s in range(2):
        for ref, col in ((gain_ref, gcol), (bias_ref, bcol)):
            value = jnp.sum(jnp.where(diagonal, ref[s : s + 1, :], 0.0), axis=1, keepdims=True)
            col[s] = jnp.broadcast_to(value, (F, 128))

    total = n * T
    for b in range(T // W):
        q_pos = root + b * W + lax.broadcasted_iota(jnp.int32, (W, 3 * W), 0)
        k_pos = root + (b - 1) * W + lax.broadcasted_iota(jnp.int32, (W, 3 * W), 1)
        low = jnp.maximum(q_pos - W, jnp.where(q_pos >= split, split, 0))
        high = jnp.minimum(q_pos + W + 1, jnp.where(q_pos >= split, total, split))
        nbias[b] = jnp.where((k_pos >= low) & (k_pos < high), 0.0, LOW)

    cp_q.wait()

    @pl.when(me > 0)
    def _():
        up.wait_recv()

    @pl.when(me < n - 1)
    def _():
        down.wait_recv()

    half = lax.broadcasted_iota(jnp.int32, (1, 2 * DH), 1) // DH

    def query(h, start, size):
        p = h // 2
        q = qv[start : start + size, p * 2 * DH : (p + 1) * 2 * DH] * jnp.asarray(0.125, BF16)
        return jnp.where(half == h % 2, q, jnp.zeros((), BF16))

    def near(h):
        p = h // 2
        lanes = slice(p * 2 * DH, (p + 1) * 2 * DH)
        for b in range(T // W):
            keys = kvx[0, b * W : (b + 3) * W, lanes]
            values = kvx[1, b * W : (b + 3) * W, lanes]
            scores = lax.dot_general(query(h, b * W, W), keys, NT, preferred_element_type=F32)
            scores = scores + nbias[b]
            top = jnp.max(scores, axis=1, keepdims=True)
            weight = jnp.exp(scores - top)
            at = slice(b * W, (b + 1) * W)
            nmax[h, at] = top
            nsum[h, at] = jnp.sum(weight, axis=1, keepdims=True)
            nacc[h, at] = jnp.dot(weight.astype(BF16), values, preferred_element_type=F32)

    for h in range(heads):
        query_all = query(h, 0, T)
        zero = jnp.zeros((), BF16)
        qdoc[h, :, 0 : 2 * DH] = jnp.where(second, zero, query_all)
        qdoc[h, :, 2 * DH : 4 * DH] = jnp.where(second, query_all, zero)
        near(h)

    mine = me // stride
    pair = me + 1 - 2 * lax.rem(me, 2)

    def own_block(d, to):
        return remote(
            tab.at[mine], tab.at[mine], tab_send.at[d], tab_recv.at[mine], to, c
        )

    def reduce_block():
        rbuf[0] = part[mine]
        rtop[0] = tops[mine]

        def wait_in(d, top):
            remote(
                tops.at[0], rtop.at[d], top_send.at[0], top_recv.at[d], me, pc
            ).wait_recv()
            remote(
                part.at[0], rbuf.at[d], part_send.at[0], part_recv.at[d], me, pc
            ).wait_recv()
            return jnp.maximum(top, rtop[d])

        top = lax.fori_loop(1, n, wait_in, rtop[0], unroll=n <= 8)[0:1]

        def add(d, running):
            scale = jnp.exp(rtop[d][0:1] - top)
            return running + rbuf[d].astype(F32) * scale[None]

        summed = lax.fori_loop(0, n, add, jnp.zeros((2, DH, R), F32), unroll=n <= 8)
        centred = summed - jnp.mean(summed, axis=1, keepdims=True)
        variance = jnp.mean(centred * centred, axis=1, keepdims=True)
        scaled = centred * lax.rsqrt(variance + EPSILON)
        at = pl.ds(pl.multiple_of(lax.rem(mine, heads) * DH, DH), DH)
        for s in range(2):
            gain = gcol[s, at, :][:, 0:1]
            bias = bcol[s, at, :][:, 0:1]
            tab[mine, s] = (scaled[s] * gain + bias).astype(BF16)

        def spread(d, carry):
            own_block(d, lax.rem(me + 2 * d, n)).start()
            return carry

        lax.fori_loop(1, n // 2, spread, 0)
        own_block(0, pair).start()

    def finish_spread():
        def done(d, carry):
            own_block(d, lax.rem(me + 2 * d, n)).wait_send()
            return carry

        lax.fori_loop(1, n // 2, done, 0)
        own_block(0, pair).wait_send()

    if stride == 1 and n == blocks:
        reduce_block()
    else:
        pl.when((lax.rem(me, stride) == 0) & (mine < blocks))(reduce_block)

    handed = []
    for b in range(blocks):
        owner = b * stride
        hand = remote(tab.at[b], tab.at[b], hand_send.at[b], tab_recv.at[b], pair, c)
        here = (me != owner) & (lax.rem(me + owner, 2) == 0)
        handed.append((hand, here))

        @pl.when(here)
        def _():
            hand.wait_recv()
            hand.start()

    for b in range(blocks):
        hand, _ = handed[b]

        @pl.when(lax.rem(me + b * stride, 2) == 1)
        def _():
            hand.wait_recv()

    for p in range(heads // 2):
        keys, values = [
            jnp.concatenate(
                [
                    tab[g * heads + 2 * p : g * heads + 2 * p + 2, s].reshape(2 * DH, R)
                    for g in range(DOCS)
                ],
                axis=0,
            )
            for s in range(2)
        ]
        halves = []
        for h in (2 * p, 2 * p + 1):
            scores = jnp.dot(qdoc[h], keys, preferred_element_type=F32)
            near_top = nmax[h]
            top = jnp.maximum(near_top, jnp.max(scores, axis=1, keepdims=True))
            weight = jnp.exp(scores - top)
            shrink = jnp.exp(near_top - top)
            denominator = nsum[h] * shrink + jnp.sum(weight, axis=1, keepdims=True)
            both = lax.dot_general(
                weight.astype(BF16), values, NT, preferred_element_type=F32
            )
            result = nacc[h] * shrink + jnp.where(
                second, both[:, 2 * DH : 4 * DH], both[:, 0 : 2 * DH]
            )
            halves.append(result / denominator)
        out_ref[:, p * 2 * DH : (p + 1) * 2 * DH] = jnp.where(
            half == 0, halves[0], halves[1]
        ).astype(out_ref.dtype)

    for _, _, cp in far:
        cp.wait_send()
    cp_pair.wait_send()
    for cp2 in fwd:
        cp2.wait_send()

    @pl.when(me < n - 1)
    def _():
        up.wait_send()

    @pl.when(me > 0)
    def _():
        down.wait_send()

    for hand, here in handed:
        pl.when(here)(hand.wait_send)

    for owner, send_top, send_part in sends:
        @pl.when(me != owner)
        def _():
            send_top.wait_send()
            send_part.wait_send()

    if stride == 1 and n == blocks:
        finish_spread()
    else:
        pl.when((lax.rem(me, stride) == 0) & (mine < blocks))(finish_spread)


def on_device(n, nd, inputs, queries, keys_values, slot_weight, slot_gain, slot_bias, bounds):
    T, F = inputs.shape
    heads = queries.shape[1] // DH
    blocks = DOCS * heads
    DMA = pltpu.SemaphoreType.DMA
    hbm = pl.BlockSpec(memory_space=pltpu.HBM)
    vmem = pl.BlockSpec(memory_space=pltpu.VMEM)
    return pl.pallas_call(
        functools.partial(kernel, n, nd),
        out_shape=jax.ShapeDtypeStruct(queries.shape, BF16),
        in_specs=[hbm] * 7,
        out_specs=vmem,
        scratch_shapes=[
            pltpu.VMEM(slot_gain.shape, F32),
            pltpu.VMEM(slot_bias.shape, F32),
            pltpu.VMEM(bounds.shape, jnp.int32),
            pltpu.VMEM((nd, T, F), BF16),
            pltpu.VMEM(slot_weight.shape, BF16),
            pltpu.VMEM(queries.shape, BF16),
            pltpu.VMEM((2, T + 2 * W, F), BF16),
            pltpu.VMEM((heads, DOCS, 2, DH, T), BF16),
            pltpu.VMEM((T, heads * R), F32),
            pltpu.VMEM((blocks, 2, DH, R), BF16),
            pltpu.VMEM((blocks, 8, R), F32),
            pltpu.VMEM((n, 2, DH, R), BF16),
            pltpu.VMEM((n, 8, R), F32),
            pltpu.VMEM((blocks, 2, DH, R), BF16),
            pltpu.VMEM((2, F, 128), F32),
            pltpu.VMEM((2, F, 128), F32),
            pltpu.VMEM((T // W, W, 3 * W), F32),
            pltpu.VMEM((heads, T, 2 * DH), F32),
            pltpu.VMEM((heads, T, 1), F32),
            pltpu.VMEM((heads, T, 1), F32),
            DMA((7,)),
            DMA((nd, CHUNKS)), DMA((nd, CHUNKS)),
            DMA, DMA,
            DMA((nd, CHUNKS)), DMA((nd, CHUNKS)),
            DMA((2,)), DMA((2,)),
            DMA((blocks,)), DMA((n,)),
            DMA((blocks,)), DMA((n,)),
            DMA((n,)), DMA((blocks,)), DMA((blocks,)),
            pltpu.VMEM((heads, T, 4 * DH), BF16),
        ],
        compiler_params=pltpu.CompilerParams(
            collective_id=0, has_side_effects=True, vmem_limit_bytes=60 * 1024 * 1024
        ),
        cost_estimate=pl.CostEstimate(
            flops=4 * 10**9, bytes_accessed=4 * 10**6, transcendentals=2 * 10**6
        ),
    )(inputs, queries, keys_values, slot_weight, slot_gain, slot_bias, bounds)


def solution(mesh):
    return jax.shard_map(
        functools.partial(on_device, mesh.shape["seq"], mesh.shape["doc"]),
        mesh=mesh,
        in_specs=(
            P("seq", "doc"),
            P("seq", "doc"),
            P(None, "seq", "doc"),
            P(None, "doc"),
            P(None, "doc"),
            P(None, "doc"),
            P(None, "seq"),
        ),
        out_specs=P("seq", "doc"),
        check_vma=False,
    )
```

```python
import functools

import jax
import jax.numpy as jnp
from jax import lax
from jax.experimental import pallas as pl
from jax.experimental.pallas import tpu as pltpu
from jax.sharding import PartitionSpec as P

DH = 64
R = 256
W = 128
DOCS = 2
CHUNKS = 2
EPSILON = 1e-05
LOW = -1e30
ZONES = 4
MESH = pl.DeviceIdType.MESH
F32 = jnp.float32
BF16 = jnp.bfloat16

NT = (((1,), (1,)), ((), ()))


def kernel(
    n, nd, zone,
    x_ref, q_ref, kv_ref, w_ref, gain_hbm, bias_hbm, bounds_hbm,
    out_ref,
    gain_ref, bias_ref, bounds_ref,
    xg, wv, qv, kvx, kvm, acc, part, tops, rbuf, rtop, tab,
    gcol, bcol, nbias, nacc, nmax, nsum,
    loc_sem, far_send, far_recv, pair_send, pair_recv, fwd_send, fwd_recv,
    halo_send, halo_recv, part_send, part_recv, top_send, top_recv,
    tab_send, tab_recv, qdoc,
):
    T, F = x_ref.shape
    heads = q_ref.shape[1] // DH
    blocks = DOCS * heads
    stride = n // blocks
    me = lax.axis_index("seq")
    c = lax.axis_index("doc")
    pc = c + 1 - 2 * lax.rem(c, 2)
    rows = T // CHUNKS

    def holds(g, device):
        return (device // (n // ZONES) - zone) * (1 - 2 * g) <= 0

    barrier = pltpu.get_barrier_semaphore()

    def greet(d, carry):
        pl.semaphore_signal(
            barrier, inc=1, device_id={"seq": lax.rem(me + d, n), "doc": c}, device_id_type=MESH
        )
        return carry

    lax.fori_loop(1, n, greet, 0)
    for d in range(1, nd):
        pl.semaphore_signal(
            barrier, inc=1, device_id={"seq": me, "doc": lax.rem(c + d, nd)}, device_id_type=MESH
        )

    cp_x = pltpu.make_async_copy(x_ref, xg.at[c], loc_sem.at[0])
    cp_w = pltpu.make_async_copy(w_ref, wv, loc_sem.at[1])
    cp_q = pltpu.make_async_copy(q_ref, qv, loc_sem.at[2])
    cp_kv = pltpu.make_async_copy(kv_ref, kvx.at[:, pl.ds(W, T), :], loc_sem.at[3])
    cp_bounds = pltpu.make_async_copy(bounds_hbm, bounds_ref, loc_sem.at[4])
    cp_gain = pltpu.make_async_copy(gain_hbm, gain_ref, loc_sem.at[5])
    cp_bias = pltpu.make_async_copy(bias_hbm, bias_ref, loc_sem.at[6])
    for cp in (cp_x, cp_w, cp_bounds, cp_kv, cp_q, cp_gain, cp_bias):
        cp.start()

    pl.semaphore_wait(barrier, n - 1 + nd - 1)

    def remote(src, dst, send, recv, seq, doc):
        return pltpu.make_async_remote_copy(
            src_ref=src, dst_ref=dst, send_sem=send, recv_sem=recv,
            device_id={"seq": seq, "doc": doc}, device_id_type=MESH,
        )

    far = []
    for k in range(1, nd // 2):
        for j in range(CHUNKS):
            part_rows = pl.ds(j * rows, rows)
            cp = remote(
                x_ref.at[part_rows], xg.at[c, part_rows],
                far_send.at[k, j], far_recv.at[k, j], me, lax.rem(c + 2 * k, nd),
            )
            cp.start()
            far.append((k, j, cp))
    cp_pair = remote(x_ref, xg.at[c], pair_send, pair_recv, me, pc)
    cp_pair.start()

    up = remote(
        kv_ref.at[:, pl.ds(T - W, W), :], kvx.at[:, pl.ds(0, W), :],
        halo_send.at[0], halo_recv.at[0], lax.rem(me + 1, n), c,
    )
    down = remote(
        kv_ref.at[:, pl.ds(0, W), :], kvx.at[:, pl.ds(T + W, W), :],
        halo_send.at[1], halo_recv.at[1], lax.rem(me + n - 1, n), c,
    )

    @pl.when(me < n - 1)
    def _():
        up.start()

    @pl.when(me > 0)
    def _():
        down.start()

    @pl.when(me == 0)
    def _():
        kvx[:, 0:W, :] = jnp.zeros((2, W, F), BF16)

    @pl.when(me == n - 1)
    def _():
        kvx[:, T + W : T + 2 * W, :] = jnp.zeros((2, W, F), BF16)

    cp_bounds.wait()
    lower = bounds_ref[0:1, 0:1]
    split = jnp.where(lower > 0, lower, bounds_ref[1:2, 0:1])
    root = me * T
    row_pos = root + lax.broadcasted_iota(jnp.int32, (T, 1), 0)
    second = row_pos >= split

    def w_rows(i):
        return wv[pl.ds(pl.multiple_of(i * F, F), F), :]

    cp_x.wait()
    cp_w.wait()
    acc[...] = jnp.dot(xg[c], w_rows(c), preferred_element_type=F32)
    cp_pair.wait_recv()
    acc[...] += jnp.dot(xg[pc], w_rows(pc), preferred_element_type=F32)

    cp_kv.wait()
    lane_pos = root + lax.broadcasted_iota(jnp.int32, (1, T), 1)
    lane_second = lane_pos >= split
    for s in range(2):
        turned = jnp.transpose(kvx[s, W : W + T, :].astype(F32))
        first_doc = jnp.where(lane_second, 0.0, turned).astype(BF16)
        other_doc = jnp.where(lane_second, turned, 0.0).astype(BF16)
        for h in range(heads):
            kvm[h, 0, s] = first_doc[h * DH : (h + 1) * DH]
            kvm[h, 1, s] = other_doc[h * DH : (h + 1) * DH]

    fwd = []
    for k, j, cp in far:
        cp.wait_recv()
        src = lax.rem(c - 2 * k + nd, nd)
        part_rows = pl.ds(j * rows, rows)
        cp2 = remote(
            xg.at[src, part_rows], xg.at[src, part_rows],
            fwd_send.at[k, j], fwd_recv.at[k, j], me, pc,
        )
        cp2.start()
        fwd.append(cp2)
    for k in range(1, nd // 2):
        src = lax.rem(c - 2 * k + nd, nd)
        acc[...] += jnp.dot(xg[src], w_rows(src), preferred_element_type=F32)
    for cp2 in fwd:
        cp2.wait_recv()
    for k in range(1, nd // 2):
        src = lax.rem(pc - 2 * k + nd, nd)
        acc[...] += jnp.dot(xg[src], w_rows(src), preferred_element_type=F32)

    sends = []
    for h in range(heads):
        logits = acc[:, h * R : (h + 1) * R]
        top0 = jnp.max(jnp.where(second, LOW, logits), axis=0, keepdims=True)
        top1 = jnp.max(jnp.where(second, logits, LOW), axis=0, keepdims=True)
        proj = jnp.exp(logits - jnp.where(second, top1, top0)).astype(BF16)
        sums = jnp.dot(
            kvm[h].reshape(DOCS * 2 * DH, T), proj, preferred_element_type=F32
        ).reshape(DOCS, 2, DH, R)
        sums = sums - jnp.mean(sums, axis=2, keepdims=True)
        for g, top in ((0, top0), (1, top1)):
            b = g * heads + h
            owner = b * stride
            slot = lax.rem(me - owner + n, n)
            tops[b] = jnp.broadcast_to(top, (8, R))
            part[b] = sums[g].astype(BF16)
            send_top = remote(
                tops.at[b], rtop.at[slot], top_send.at[b], top_recv.at[slot], owner, c
            )
            send_part = remote(
                part.at[b], rbuf.at[slot], part_send.at[b], part_recv.at[slot], owner, c
            )
            out = (me != owner) & holds(g, me)
            sends.append((out, send_top, send_part))

            @pl.when(out)
            def _():
                send_top.start()
                send_part.start()

    cp_gain.wait()
    cp_bias.wait()
    diagonal = lax.broadcasted_iota(jnp.int32, (F, F), 0) == lax.broadcasted_iota(
        jnp.int32, (F, F), 1
    )
    for s in range(2):
        for ref, col in ((gain_ref, gcol), (bias_ref, bcol)):
            value = jnp.sum(jnp.where(diagonal, ref[s : s + 1, :], 0.0), axis=1, keepdims=True)
            col[s] = jnp.broadcast_to(value, (F, 128))

    total = n * T
    for b in range(T // W):
        q_pos = root + b * W + lax.broadcasted_iota(jnp.int32, (W, 3 * W), 0)
        k_pos = root + (b - 1) * W + lax.broadcasted_iota(jnp.int32, (W, 3 * W), 1)
        low = jnp.maximum(q_pos - W, jnp.where(q_pos >= split, split, 0))
        high = jnp.minimum(q_pos + W + 1, jnp.where(q_pos >= split, total, split))
        nbias[b] = jnp.where((k_pos >= low) & (k_pos < high), 0.0, LOW)

    cp_q.wait()

    @pl.when(me > 0)
    def _():
        up.wait_recv()

    @pl.when(me < n - 1)
    def _():
        down.wait_recv()

    half = lax.broadcasted_iota(jnp.int32, (1, 2 * DH), 1) // DH

    def query(h, start, size):
        p = h // 2
        q = qv[start : start + size, p * 2 * DH : (p + 1) * 2 * DH] * jnp.asarray(0.125, BF16)
        return jnp.where(half == h % 2, q, jnp.zeros((), BF16))

    def near(h):
        p = h // 2
        lanes = slice(p * 2 * DH, (p + 1) * 2 * DH)
        for b in range(T // W):
            keys = kvx[0, b * W : (b + 3) * W, lanes]
            values = kvx[1, b * W : (b + 3) * W, lanes]
            scores = lax.dot_general(query(h, b * W, W), keys, NT, preferred_element_type=F32)
            scores = scores + nbias[b]
            top = jnp.max(scores, axis=1, keepdims=True)
            weight = jnp.exp(scores - top)
            at = slice(b * W, (b + 1) * W)
            nmax[h, at] = top
            nsum[h, at] = jnp.sum(weight, axis=1, keepdims=True)
            nacc[h, at] = jnp.dot(weight.astype(BF16), values, preferred_element_type=F32)

    for h in range(heads):
        query_all = query(h, 0, T)
        zero = jnp.zeros((), BF16)
        qdoc[h, :, 0 : 2 * DH] = jnp.where(second, zero, query_all)
        qdoc[h, :, 2 * DH : 4 * DH] = jnp.where(second, query_all, zero)
        near(h)

    mine = me // stride
    doc_mine = mine // heads

    def own_block(d):
        return remote(
            tab.at[mine], tab.at[mine], tab_send.at[d], tab_recv.at[mine],
            lax.rem(me + d, n), c,
        )

    def reduce_block():
        rbuf[0] = part[mine]
        rtop[0] = tops[mine]

        def wait_in(d, top):
            held = holds(doc_mine, lax.rem(me + d, n))

            @pl.when(held)
            def _():
                remote(
                    tops.at[0], rtop.at[d], top_send.at[0], top_recv.at[d], me, pc
                ).wait_recv()
                remote(
                    part.at[0], rbuf.at[d], part_send.at[0], part_recv.at[d], me, pc
                ).wait_recv()

            @pl.when(jnp.logical_not(held))
            def _():
                rtop[d] = jnp.full((8, R), LOW, F32)
                rbuf[d] = jnp.zeros((2, DH, R), BF16)

            return jnp.maximum(top, rtop[d])

        top = lax.fori_loop(1, n, wait_in, rtop[0], unroll=n <= 8)[0:1]

        def add(d, running):
            scale = jnp.exp(rtop[d][0:1] - top)
            return running + rbuf[d].astype(F32) * scale[None]

        summed = lax.fori_loop(0, n, add, jnp.zeros((2, DH, R), F32), unroll=n <= 8)
        centred = summed - jnp.mean(summed, axis=1, keepdims=True)
        variance = jnp.mean(centred * centred, axis=1, keepdims=True)
        scaled = centred * lax.rsqrt(variance + EPSILON)
        at = pl.ds(pl.multiple_of(lax.rem(mine, heads) * DH, DH), DH)
        for s in range(2):
            gain = gcol[s, at, :][:, 0:1]
            bias = bcol[s, at, :][:, 0:1]
            tab[mine, s] = (scaled[s] * gain + bias).astype(BF16)

        def spread(d, carry):
            pl.when(holds(doc_mine, lax.rem(me + d, n)))(own_block(d).start)
            return carry

        lax.fori_loop(1, n, spread, 0)

    def finish_spread():
        def done(d, carry):
            pl.when(holds(doc_mine, lax.rem(me + d, n)))(own_block(d).wait_send)
            return carry

        lax.fori_loop(1, n, done, 0)

    if stride == 1 and n == blocks:
        reduce_block()
    else:
        pl.when((lax.rem(me, stride) == 0) & (mine < blocks))(reduce_block)

    for b in range(blocks):
        held = holds(b // heads, me)

        @pl.when((me != b * stride) & held)
        def _():
            remote(
                tab.at[b], tab.at[b], tab_send.at[0], tab_recv.at[b], me, pc
            ).wait_recv()

        @pl.when((me != b * stride) & jnp.logical_not(held))
        def _():
            tab[b] = jnp.zeros((2, DH, R), BF16)

    for p in range(heads // 2):
        keys, values = [
            jnp.concatenate(
                [
                    tab[g * heads + 2 * p : g * heads + 2 * p + 2, s].reshape(2 * DH, R)
                    for g in range(DOCS)
                ],
                axis=0,
            )
            for s in range(2)
        ]
        halves = []
        for h in (2 * p, 2 * p + 1):
            scores = jnp.dot(qdoc[h], keys, preferred_element_type=F32)
            near_top = nmax[h]
            top = jnp.maximum(near_top, jnp.max(scores, axis=1, keepdims=True))
            weight = jnp.exp(scores - top)
            shrink = jnp.exp(near_top - top)
            denominator = nsum[h] * shrink + jnp.sum(weight, axis=1, keepdims=True)
            both = lax.dot_general(
                weight.astype(BF16), values, NT, preferred_element_type=F32
            )
            result = nacc[h] * shrink + jnp.where(
                second, both[:, 2 * DH : 4 * DH], both[:, 0 : 2 * DH]
            )
            halves.append(result / denominator)
        out_ref[:, p * 2 * DH : (p + 1) * 2 * DH] = jnp.where(
            half == 0, halves[0], halves[1]
        ).astype(out_ref.dtype)

    for _, _, cp in far:
        cp.wait_send()
    cp_pair.wait_send()
    for cp2 in fwd:
        cp2.wait_send()

    @pl.when(me < n - 1)
    def _():
        up.wait_send()

    @pl.when(me > 0)
    def _():
        down.wait_send()

    for out, send_top, send_part in sends:
        @pl.when(out)
        def _():
            send_top.wait_send()
            send_part.wait_send()

    if stride == 1 and n == blocks:
        finish_spread()
    else:
        pl.when((lax.rem(me, stride) == 0) & (mine < blocks))(finish_spread)


def on_device(n, nd, inputs, queries, keys_values, slot_weight, slot_gain, slot_bias, bounds):
    T, F = inputs.shape
    heads = queries.shape[1] // DH
    blocks = DOCS * heads
    DMA = pltpu.SemaphoreType.DMA
    hbm = pl.BlockSpec(memory_space=pltpu.HBM)
    vmem = pl.BlockSpec(memory_space=pltpu.VMEM)
    call = lambda zone: pl.pallas_call(
        functools.partial(kernel, n, nd, zone),
        out_shape=jax.ShapeDtypeStruct(queries.shape, BF16),
        in_specs=[hbm] * 7,
        out_specs=vmem,
        scratch_shapes=[
            pltpu.VMEM(slot_gain.shape, F32),
            pltpu.VMEM(slot_bias.shape, F32),
            pltpu.VMEM(bounds.shape, jnp.int32),
            pltpu.VMEM((nd, T, F), BF16),
            pltpu.VMEM(slot_weight.shape, BF16),
            pltpu.VMEM(queries.shape, BF16),
            pltpu.VMEM((2, T + 2 * W, F), BF16),
            pltpu.VMEM((heads, DOCS, 2, DH, T), BF16),
            pltpu.VMEM((T, heads * R), F32),
            pltpu.VMEM((blocks, 2, DH, R), BF16),
            pltpu.VMEM((blocks, 8, R), F32),
            pltpu.VMEM((n, 2, DH, R), BF16),
            pltpu.VMEM((n, 8, R), F32),
            pltpu.VMEM((blocks, 2, DH, R), BF16),
            pltpu.VMEM((2, F, 128), F32),
            pltpu.VMEM((2, F, 128), F32),
            pltpu.VMEM((T // W, W, 3 * W), F32),
            pltpu.VMEM((heads, T, 2 * DH), F32),
            pltpu.VMEM((heads, T, 1), F32),
            pltpu.VMEM((heads, T, 1), F32),
            DMA((7,)),
            DMA((nd, CHUNKS)), DMA((nd, CHUNKS)),
            DMA, DMA,
            DMA((nd, CHUNKS)), DMA((nd, CHUNKS)),
            DMA((2,)), DMA((2,)),
            DMA((blocks,)), DMA((n,)),
            DMA((blocks,)), DMA((n,)),
            DMA((n,)), DMA((blocks,)),
            pltpu.VMEM((heads, T, 4 * DH), BF16),
        ],
        compiler_params=pltpu.CompilerParams(
            collective_id=zone, has_side_effects=True, vmem_limit_bytes=60 * 1024 * 1024
        ),
        cost_estimate=pl.CostEstimate(
            flops=4 * 10**9, bytes_accessed=4 * 10**6, transcendentals=2 * 10**6
        ),
    )
    lower = bounds[0, 0]
    split = jnp.where(lower > 0, lower, bounds[1, 0])
    return lax.cond(
        split <= n * T // 2, call(1), call(2),
        inputs, queries, keys_values, slot_weight, slot_gain, slot_bias, bounds,
    )


def solution(mesh):
    return jax.shard_map(
        functools.partial(on_device, mesh.shape["seq"], mesh.shape["doc"]),
        mesh=mesh,
        in_specs=(
            P("seq", "doc"),
            P("seq", "doc"),
            P(None, "seq", "doc"),
            P(None, "doc"),
            P(None, "doc"),
            P(None, "doc"),
            P(None, "seq"),
        ),
        out_specs=P("seq", "doc"),
        check_vma=False,
    )
```

```python
import functools

import jax
import jax.numpy as jnp
from jax import lax
from jax.experimental import pallas as pl
from jax.experimental.pallas import tpu as pltpu
from jax.sharding import PartitionSpec as P

DH = 64
R = 256
W = 128
DOCS = 2
CHUNKS = 2
EPSILON = 1e-05
LOW = -1e30
ZONES = 4
MESH = pl.DeviceIdType.MESH
F32 = jnp.float32
BF16 = jnp.bfloat16

NT = (((1,), (1,)), ((), ()))


def kernel(
    n, nd, zone,
    x_ref, q_ref, kv_ref, w_ref, gain_hbm, bias_hbm, bounds_hbm,
    out_ref,
    gain_ref, bias_ref, bounds_ref,
    xg, wv, qv, kvx, kvm, acc, part, tops, rbuf, rtop, tab,
    gcol, bcol, nbias, nacc, nmax, nsum,
    loc_sem, far_send, far_recv, pair_send, pair_recv, fwd_send, fwd_recv,
    halo_send, halo_recv, part_send, part_recv, top_send, top_recv,
    tab_send, tab_recv, qdoc,
):
    T, F = x_ref.shape
    heads = q_ref.shape[1] // DH
    blocks = DOCS * heads
    stride = n // blocks
    me = lax.axis_index("seq")
    c = lax.axis_index("doc")
    pc = c + 1 - 2 * lax.rem(c, 2)
    rows = T // CHUNKS

    def holds(g, device):
        return (device // (n // ZONES) - zone) * (1 - 2 * g) <= 0

    barrier = pltpu.get_barrier_semaphore()

    def greet(d, carry):
        pl.semaphore_signal(
            barrier, inc=1, device_id={"seq": lax.rem(me + d, n), "doc": c}, device_id_type=MESH
        )
        return carry

    lax.fori_loop(1, n, greet, 0)
    for d in range(1, nd):
        pl.semaphore_signal(
            barrier, inc=1, device_id={"seq": me, "doc": lax.rem(c + d, nd)}, device_id_type=MESH
        )

    cp_x = pltpu.make_async_copy(x_ref, xg.at[c], loc_sem.at[0])
    cp_w = pltpu.make_async_copy(w_ref, wv, loc_sem.at[1])
    cp_q = pltpu.make_async_copy(q_ref, qv, loc_sem.at[2])
    cp_kv = pltpu.make_async_copy(kv_ref, kvx.at[:, pl.ds(W, T), :], loc_sem.at[3])
    cp_bounds = pltpu.make_async_copy(bounds_hbm, bounds_ref, loc_sem.at[4])
    cp_gain = pltpu.make_async_copy(gain_hbm, gain_ref, loc_sem.at[5])
    cp_bias = pltpu.make_async_copy(bias_hbm, bias_ref, loc_sem.at[6])
    for cp in (cp_x, cp_w, cp_bounds, cp_kv, cp_q, cp_gain, cp_bias):
        cp.start()

    pl.semaphore_wait(barrier, n - 1 + nd - 1)

    def remote(src, dst, send, recv, seq, doc):
        return pltpu.make_async_remote_copy(
            src_ref=src, dst_ref=dst, send_sem=send, recv_sem=recv,
            device_id={"seq": seq, "doc": doc}, device_id_type=MESH,
        )

    far = []
    for k in range(1, nd // 2):
        for j in range(CHUNKS):
            part_rows = pl.ds(j * rows, rows)
            cp = remote(
                x_ref.at[part_rows], xg.at[c, part_rows],
                far_send.at[k, j], far_recv.at[k, j], me, lax.rem(c + 2 * k, nd),
            )
            cp.start()
            far.append((k, j, cp))
    cp_pair = remote(x_ref, xg.at[c], pair_send, pair_recv, me, pc)
    cp_pair.start()

    up = remote(
        kv_ref.at[:, pl.ds(T - W, W), :], kvx.at[:, pl.ds(0, W), :],
        halo_send.at[0], halo_recv.at[0], lax.rem(me + 1, n), c,
    )
    down = remote(
        kv_ref.at[:, pl.ds(0, W), :], kvx.at[:, pl.ds(T + W, W), :],
        halo_send.at[1], halo_recv.at[1], lax.rem(me + n - 1, n), c,
    )

    @pl.when(me < n - 1)
    def _():
        up.start()

    @pl.when(me > 0)
    def _():
        down.start()

    @pl.when(me == 0)
    def _():
        kvx[:, 0:W, :] = jnp.zeros((2, W, F), BF16)

    @pl.when(me == n - 1)
    def _():
        kvx[:, T + W : T + 2 * W, :] = jnp.zeros((2, W, F), BF16)

    cp_bounds.wait()
    lower = bounds_ref[0:1, 0:1]
    split = jnp.where(lower > 0, lower, bounds_ref[1:2, 0:1])
    root = me * T
    row_pos = root + lax.broadcasted_iota(jnp.int32, (T, 1), 0)
    second = row_pos >= split

    def w_rows(i):
        return wv[pl.ds(pl.multiple_of(i * F, F), F), :]

    cp_x.wait()
    cp_w.wait()
    acc[...] = jnp.dot(xg[c], w_rows(c), preferred_element_type=F32)
    cp_pair.wait_recv()
    acc[...] += jnp.dot(xg[pc], w_rows(pc), preferred_element_type=F32)

    cp_kv.wait()
    lane_pos = root + lax.broadcasted_iota(jnp.int32, (1, T), 1)
    lane_second = lane_pos >= split
    for s in range(2):
        turned = jnp.transpose(kvx[s, W : W + T, :].astype(F32))
        first_doc = jnp.where(lane_second, 0.0, turned).astype(BF16)
        other_doc = jnp.where(lane_second, turned, 0.0).astype(BF16)
        for h in range(heads):
            kvm[h, 0, s] = first_doc[h * DH : (h + 1) * DH]
            kvm[h, 1, s] = other_doc[h * DH : (h + 1) * DH]

    fwd = []
    for k, j, cp in far:
        cp.wait_recv()
        src = lax.rem(c - 2 * k + nd, nd)
        part_rows = pl.ds(j * rows, rows)
        cp2 = remote(
            xg.at[src, part_rows], xg.at[src, part_rows],
            fwd_send.at[k, j], fwd_recv.at[k, j], me, pc,
        )
        cp2.start()
        fwd.append(cp2)
    for k in range(1, nd // 2):
        src = lax.rem(c - 2 * k + nd, nd)
        acc[...] += jnp.dot(xg[src], w_rows(src), preferred_element_type=F32)
    for cp2 in fwd:
        cp2.wait_recv()
    for k in range(1, nd // 2):
        src = lax.rem(pc - 2 * k + nd, nd)
        acc[...] += jnp.dot(xg[src], w_rows(src), preferred_element_type=F32)

    sends = []
    for h in range(heads):
        logits = acc[:, h * R : (h + 1) * R]
        top0 = jnp.max(jnp.where(second, LOW, logits), axis=0, keepdims=True)
        top1 = jnp.max(jnp.where(second, logits, LOW), axis=0, keepdims=True)
        proj = jnp.exp(logits - jnp.where(second, top1, top0)).astype(BF16)
        sums = jnp.dot(
            kvm[h].reshape(DOCS * 2 * DH, T), proj, preferred_element_type=F32
        ).reshape(DOCS, 2, DH, R)
        sums = sums - jnp.mean(sums, axis=2, keepdims=True)
        for g, top in ((0, top0), (1, top1)):
            b = g * heads + h
            owner = b * stride
            slot = lax.rem(me - owner + n, n)
            tops[b] = jnp.broadcast_to(top, (8, R))
            part[b] = sums[g].astype(BF16)
            send_top = remote(
                tops.at[b], rtop.at[slot], top_send.at[b], top_recv.at[slot], owner, c
            )
            send_part = remote(
                part.at[b], rbuf.at[slot], part_send.at[b], part_recv.at[slot], owner, c
            )
            out = (me != owner) & holds(g, me)
            sends.append((out, send_top, send_part))

            @pl.when(out)
            def _():
                send_top.start()
                send_part.start()

    cp_gain.wait()
    cp_bias.wait()
    diagonal = lax.broadcasted_iota(jnp.int32, (F, F), 0) == lax.broadcasted_iota(
        jnp.int32, (F, F), 1
    )
    for s in range(2):
        for ref, col in ((gain_ref, gcol), (bias_ref, bcol)):
            value = jnp.sum(jnp.where(diagonal, ref[s : s + 1, :], 0.0), axis=1, keepdims=True)
            col[s] = jnp.broadcast_to(value, (F, 128))

    total = n * T
    for b in range(T // W):
        q_pos = root + b * W + lax.broadcasted_iota(jnp.int32, (W, 3 * W), 0)
        k_pos = root + (b - 1) * W + lax.broadcasted_iota(jnp.int32, (W, 3 * W), 1)
        low = jnp.maximum(q_pos - W, jnp.where(q_pos >= split, split, 0))
        high = jnp.minimum(q_pos + W + 1, jnp.where(q_pos >= split, total, split))
        nbias[b] = jnp.where((k_pos >= low) & (k_pos < high), 0.0, LOW)

    cp_q.wait()

    @pl.when(me > 0)
    def _():
        up.wait_recv()

    @pl.when(me < n - 1)
    def _():
        down.wait_recv()

    half = lax.broadcasted_iota(jnp.int32, (1, 2 * DH), 1) // DH

    def query(h, start, size):
        p = h // 2
        q = qv[start : start + size, p * 2 * DH : (p + 1) * 2 * DH] * jnp.asarray(0.125, BF16)
        return jnp.where(half == h % 2, q, jnp.zeros((), BF16))

    def near(h):
        p = h // 2
        lanes = slice(p * 2 * DH, (p + 1) * 2 * DH)
        for b in range(T // W):
            keys = kvx[0, b * W : (b + 3) * W, lanes]
            values = kvx[1, b * W : (b + 3) * W, lanes]
            scores = lax.dot_general(query(h, b * W, W), keys, NT, preferred_element_type=F32)
            scores = scores + nbias[b]
            top = jnp.max(scores, axis=1, keepdims=True)
            weight = jnp.exp(scores - top)
            at = slice(b * W, (b + 1) * W)
            nmax[h, at] = top
            nsum[h, at] = jnp.sum(weight, axis=1, keepdims=True)
            nacc[h, at] = jnp.dot(weight.astype(BF16), values, preferred_element_type=F32)

    for h in range(heads // 2):
        near(h)

    mine = me // stride
    doc_mine = mine // heads

    def own_block(d):
        return remote(
            tab.at[mine], tab.at[mine], tab_send.at[d], tab_recv.at[mine],
            lax.rem(me + d, n), c,
        )

    def reduce_block():
        rbuf[0] = part[mine]
        rtop[0] = tops[mine]

        def wait_in(d, top):
            held = holds(doc_mine, lax.rem(me + d, n))

            @pl.when(held)
            def _():
                remote(
                    tops.at[0], rtop.at[d], top_send.at[0], top_recv.at[d], me, pc
                ).wait_recv()
                remote(
                    part.at[0], rbuf.at[d], part_send.at[0], part_recv.at[d], me, pc
                ).wait_recv()

            @pl.when(jnp.logical_not(held))
            def _():
                rtop[d] = jnp.full((8, R), LOW, F32)
                rbuf[d] = jnp.zeros((2, DH, R), BF16)

            return jnp.maximum(top, rtop[d])

        top = lax.fori_loop(1, n, wait_in, rtop[0], unroll=n <= 8)[0:1]

        def add(d, running):
            scale = jnp.exp(rtop[d][0:1] - top)
            return running + rbuf[d].astype(F32) * scale[None]

        summed = lax.fori_loop(0, n, add, jnp.zeros((2, DH, R), F32), unroll=n <= 8)
        centred = summed - jnp.mean(summed, axis=1, keepdims=True)
        variance = jnp.mean(centred * centred, axis=1, keepdims=True)
        scaled = centred * lax.rsqrt(variance + EPSILON)
        at = pl.ds(pl.multiple_of(lax.rem(mine, heads) * DH, DH), DH)
        for s in range(2):
            gain = gcol[s, at, :][:, 0:1]
            bias = bcol[s, at, :][:, 0:1]
            tab[mine, s] = (scaled[s] * gain + bias).astype(BF16)

        def spread(d, carry):
            pl.when(holds(doc_mine, lax.rem(me + d, n)))(own_block(d).start)
            return carry

        lax.fori_loop(1, n, spread, 0)

    def finish_spread():
        def done(d, carry):
            pl.when(holds(doc_mine, lax.rem(me + d, n)))(own_block(d).wait_send)
            return carry

        lax.fori_loop(1, n, done, 0)

    if stride == 1 and n == blocks:
        reduce_block()
    else:
        pl.when((lax.rem(me, stride) == 0) & (mine < blocks))(reduce_block)

    for h in range(heads):
        query_all = query(h, 0, T)
        zero = jnp.zeros((), BF16)
        qdoc[h, :, 0 : 2 * DH] = jnp.where(second, zero, query_all)
        qdoc[h, :, 2 * DH : 4 * DH] = jnp.where(second, query_all, zero)
        if h >= heads // 2:
            near(h)

    for b in range(blocks):
        held = holds(b // heads, me)

        @pl.when((me != b * stride) & held)
        def _():
            remote(
                tab.at[b], tab.at[b], tab_send.at[0], tab_recv.at[b], me, pc
            ).wait_recv()

        @pl.when((me != b * stride) & jnp.logical_not(held))
        def _():
            tab[b] = jnp.zeros((2, DH, R), BF16)

    for p in range(heads // 2):
        keys, values = [
            jnp.concatenate(
                [
                    tab[g * heads + 2 * p : g * heads + 2 * p + 2, s].reshape(2 * DH, R)
                    for g in range(DOCS)
                ],
                axis=0,
            )
            for s in range(2)
        ]
        halves = []
        for h in (2 * p, 2 * p + 1):
            scores = jnp.dot(qdoc[h], keys, preferred_element_type=F32)
            near_top = nmax[h]
            top = jnp.maximum(near_top, jnp.max(scores, axis=1, keepdims=True))
            weight = jnp.exp(scores - top)
            shrink = jnp.exp(near_top - top)
            denominator = nsum[h] * shrink + jnp.sum(weight, axis=1, keepdims=True)
            both = lax.dot_general(
                weight.astype(BF16), values, NT, preferred_element_type=F32
            )
            result = nacc[h] * shrink + jnp.where(
                second, both[:, 2 * DH : 4 * DH], both[:, 0 : 2 * DH]
            )
            halves.append(result / denominator)
        out_ref[:, p * 2 * DH : (p + 1) * 2 * DH] = jnp.where(
            half == 0, halves[0], halves[1]
        ).astype(out_ref.dtype)

    for _, _, cp in far:
        cp.wait_send()
    cp_pair.wait_send()
    for cp2 in fwd:
        cp2.wait_send()

    @pl.when(me < n - 1)
    def _():
        up.wait_send()

    @pl.when(me > 0)
    def _():
        down.wait_send()

    for out, send_top, send_part in sends:
        @pl.when(out)
        def _():
            send_top.wait_send()
            send_part.wait_send()

    if stride == 1 and n == blocks:
        finish_spread()
    else:
        pl.when((lax.rem(me, stride) == 0) & (mine < blocks))(finish_spread)


def on_device(n, nd, inputs, queries, keys_values, slot_weight, slot_gain, slot_bias, bounds):
    T, F = inputs.shape
    heads = queries.shape[1] // DH
    blocks = DOCS * heads
    DMA = pltpu.SemaphoreType.DMA
    hbm = pl.BlockSpec(memory_space=pltpu.HBM)
    vmem = pl.BlockSpec(memory_space=pltpu.VMEM)
    call = lambda zone: pl.pallas_call(
        functools.partial(kernel, n, nd, zone),
        out_shape=jax.ShapeDtypeStruct(queries.shape, BF16),
        in_specs=[hbm] * 7,
        out_specs=vmem,
        scratch_shapes=[
            pltpu.VMEM(slot_gain.shape, F32),
            pltpu.VMEM(slot_bias.shape, F32),
            pltpu.VMEM(bounds.shape, jnp.int32),
            pltpu.VMEM((nd, T, F), BF16),
            pltpu.VMEM(slot_weight.shape, BF16),
            pltpu.VMEM(queries.shape, BF16),
            pltpu.VMEM((2, T + 2 * W, F), BF16),
            pltpu.VMEM((heads, DOCS, 2, DH, T), BF16),
            pltpu.VMEM((T, heads * R), F32),
            pltpu.VMEM((blocks, 2, DH, R), BF16),
            pltpu.VMEM((blocks, 8, R), F32),
            pltpu.VMEM((n, 2, DH, R), BF16),
            pltpu.VMEM((n, 8, R), F32),
            pltpu.VMEM((blocks, 2, DH, R), BF16),
            pltpu.VMEM((2, F, 128), F32),
            pltpu.VMEM((2, F, 128), F32),
            pltpu.VMEM((T // W, W, 3 * W), F32),
            pltpu.VMEM((heads, T, 2 * DH), F32),
            pltpu.VMEM((heads, T, 1), F32),
            pltpu.VMEM((heads, T, 1), F32),
            DMA((7,)),
            DMA((nd, CHUNKS)), DMA((nd, CHUNKS)),
            DMA, DMA,
            DMA((nd, CHUNKS)), DMA((nd, CHUNKS)),
            DMA((2,)), DMA((2,)),
            DMA((blocks,)), DMA((n,)),
            DMA((blocks,)), DMA((n,)),
            DMA((n,)), DMA((blocks,)),
            pltpu.VMEM((heads, T, 4 * DH), BF16),
        ],
        compiler_params=pltpu.CompilerParams(
            collective_id=zone, has_side_effects=True, vmem_limit_bytes=60 * 1024 * 1024
        ),
        cost_estimate=pl.CostEstimate(
            flops=4 * 10**9, bytes_accessed=4 * 10**6, transcendentals=2 * 10**6
        ),
    )
    lower = bounds[0, 0]
    split = jnp.where(lower > 0, lower, bounds[1, 0])
    return lax.cond(
        split <= n * T // 2, call(1), call(2),
        inputs, queries, keys_values, slot_weight, slot_gain, slot_bias, bounds,
    )


def solution(mesh):
    return jax.shard_map(
        functools.partial(on_device, mesh.shape["seq"], mesh.shape["doc"]),
        mesh=mesh,
        in_specs=(
            P("seq", "doc"),
            P("seq", "doc"),
            P(None, "seq", "doc"),
            P(None, "doc"),
            P(None, "doc"),
            P(None, "doc"),
            P(None, "seq"),
        ),
        out_specs=P("seq", "doc"),
        check_vma=False,
    )
```
